32 devices in a mesh: seq: 8 (over z, y), head: 4 (over x, core).
Axes of the slice: x: 2, y: 2, z: 4, core: 2. Of those that a mesh axis runs over, the one named last changes fastest.
Arguments:
- tokens: bfloat16 [16384, 1024], P(('seq', 'head')), may hold values from -6 to 6
- w_gate_x: bfloat16 [1024, 4096], replicated, may hold values from -0.1875 to 0.1875
- w_bc_dt: bfloat16 [1024, 160], replicated, may hold values from -0.1875 to 0.1875
- conv_x_weight: float32 [4, 2048], P(None, 'head'), may hold values from -0.5 to 0.5
- conv_x_bias: float32 [2048], P('head'), may hold values from -0.5 to 0.5
- conv_bc_weight: float32 [4, 128], replicated, may hold values from -0.5 to 0.5
- conv_bc_bias: float32 [128], replicated, may hold values from -0.5 to 0.5
- dt_bias: float32 [32], P('head'), may hold values from -9 to -1
- a_log: float32 [32], P('head'), may hold values from -4 to 1
- skip_d: float32 [32], P('head'), may hold values from 0.5 to 1.5
- norm_gain: float32 [2048], replicated, may hold values from 0.1 to 1.9
- w_out: bfloat16 [2048, 1024], replicated, may hold values from -0.125 to 0.125
Outputs:
- mixed: bfloat16 [16384, 1024], P(('seq', 'head'))
The draws below stay inside these ranges and needn't reach their ends.
All inputs are finite; a program needn't handle non-finite values.
Results may differ from the reference program's by a relative error of at most 0.009.
Values may be sent and summed in bfloat16 or wider, within the bound.
A program may use at most 128 MiB of HBM per device.

```python
import jax
import jax.numpy as jnp
from jax import lax

D = 1024
HEADS = 32
HEAD_DIM = 64
STATE = 64
GROUP = 256
CONV = 4
DINNER = 2048
TOKENS = 16384


def level_of(stream_key, extent, cuts, low, largest):
    gain = 1.0
    for position, shards_of in cuts:
        steps = jax.random.uniform(jax.random.fold_in(jax.random.fold_in(stream_key, 6), position), (shards_of,), jnp.float32, low / len(cuts), largest / len(cuts))
        gain = gain * jnp.repeat(jnp.exp(steps), extent[position] // shards_of).reshape((-1,) + (1,) * (len(extent) - 1 - position))
    return gain


def normal_values(own_key, shape, width, bound, pieces=(), dtype=jnp.bfloat16):
    level = level_of(own_key, shape, pieces, -0.22, 0.18) if pieces else 1.0
    result = jax.random.normal(own_key, shape, jnp.float32) * width * level
    return jnp.minimum(jnp.maximum(result, -bound), bound).astype(dtype)


def setup_inputs(seed: int = 0) -> dict:
    key_of = jax.random.split(jax.random.key(seed), 13)
    tokens = normal_values(key_of[0], (TOKENS, D), 1.0, 6.0, ((0, 32),))
    w_gate_x = normal_values(key_of[1], (D, 2 * DINNER), D ** -0.5, 0.1875)
    w_bc_dt = normal_values(key_of[2], (D, 2 * STATE + HEADS), D ** -0.5, 0.1875)
    conv_x_weight = jnp.clip(jax.random.uniform(key_of[3], (CONV, DINNER), jnp.float32, -0.5, 0.5) * level_of(key_of[3], (CONV, DINNER), ((1, 4),), -0.4, 0.0), -0.5, 0.5)
    conv_x_bias = jnp.clip(jax.random.uniform(key_of[4], (DINNER,), jnp.float32, -0.5, 0.5) * level_of(key_of[4], (DINNER,), ((0, 4),), -0.4, 0.0), -0.5, 0.5)
    conv_bc_weight = jnp.clip(jax.random.uniform(key_of[5], (CONV, 2 * STATE), jnp.float32, -0.5, 0.5), -0.5, 0.5)
    conv_bc_bias = jnp.clip(jax.random.uniform(key_of[6], (2 * STATE,), jnp.float32, -0.5, 0.5), -0.5, 0.5)
    dt_bias = jnp.clip(-9.0 + 8.0 * jax.random.uniform(key_of[7], (HEADS,), jnp.float32) ** level_of(key_of[7], (HEADS,), ((0, 4),), -0.2, 0.2), -9.0, -1.0)
    a_log = jnp.clip(-4.0 + 5.0 * jax.random.uniform(key_of[8], (HEADS,), jnp.float32) ** level_of(key_of[8], (HEADS,), ((0, 4),), -0.2, 0.2), -4.0, 1.0)
    skip_d = jnp.clip(0.5 + 1.0 * jax.random.uniform(key_of[9], (HEADS,), jnp.float32) ** level_of(key_of[9], (HEADS,), ((0, 4),), -0.2, 0.2), 0.5, 1.5)
    norm_gain = jnp.clip(1.0 + 0.18 * jax.random.normal(key_of[10], (DINNER,), jnp.float32), 0.1, 1.9)
    w_out = normal_values(key_of[11], (DINNER, D), DINNER ** -0.5, 0.125)
    return dict(tokens=tokens, w_gate_x=w_gate_x, w_bc_dt=w_bc_dt, conv_x_weight=conv_x_weight, conv_x_bias=conv_x_bias, conv_bc_weight=conv_bc_weight, conv_bc_bias=conv_bc_bias, dt_bias=dt_bias, a_log=a_log, skip_d=skip_d, norm_gain=norm_gain, w_out=w_out)


epsilon = 1e-05

def causal_taps(source, weights, biases):
    count = source.shape[0]
    padded = jnp.pad(source.astype(jnp.float32), ((CONV - 1, 0), (0, 0)))
    summed = biases + weights[0] * padded[0:count]
    for tap_index in range(1, CONV):
        summed = summed + weights[tap_index] * padded[tap_index:tap_index + count]
    return jax.nn.silu(summed).astype(jnp.bfloat16)

def reference(tokens, w_gate_x, w_bc_dt, conv_x_weight, conv_x_bias, conv_bc_weight, conv_bc_bias, dt_bias, a_log, skip_d, norm_gain, w_out):
    highest = lax.Precision.HIGHEST
    gate_x = jnp.dot(tokens, w_gate_x, preferred_element_type=jnp.float32).astype(jnp.bfloat16)
    gate_x = gate_x.reshape(TOKENS, HEADS, 2 * HEAD_DIM)
    bc_dt = jnp.dot(tokens, w_bc_dt, preferred_element_type=jnp.float32).astype(jnp.bfloat16)
    gate_z = gate_x[:, :, :HEAD_DIM]
    x_chan = gate_x[:, :, HEAD_DIM:].reshape(TOKENS, DINNER)
    conved_x = causal_taps(x_chan, conv_x_weight, conv_x_bias)
    conved_bc = causal_taps(bc_dt[:, :2 * STATE], conv_bc_weight, conv_bc_bias)
    dt_step = jax.nn.softplus(bc_dt[:, 2 * STATE:].astype(jnp.float32) + dt_bias)
    log_decay = dt_step * -jnp.exp(a_log)
    x_heads = conved_x.astype(jnp.float32).reshape(TOKENS, HEADS, HEAD_DIM)
    x_dt = x_heads * dt_step[:, :, None]
    b_mat = conved_bc[:, :STATE].astype(jnp.float32)
    c_mat = conved_bc[:, STATE:].astype(jnp.float32)
    blocks = TOKENS // GROUP
    causal = jnp.arange(GROUP)[:, None] >= jnp.arange(GROUP)[None, :]

    def group_step(carried, inputs):
        decay_c, xdt_c, b_c, c_c = inputs
        cumlog = jnp.cumsum(decay_c, axis=0)
        scores = jnp.dot(c_c, b_c.T, precision=highest)
        by_head = cumlog.T
        gaps = by_head[:, :, None] - by_head[:, None, :]
        decays = jnp.where(causal[None], jnp.exp(jnp.minimum(gaps, 0.0)), 0.0)
        mixed = scores[None] * decays
        outputs = jnp.einsum('hts,shp->thp', mixed, xdt_c, precision=highest)
        outputs = outputs + jnp.exp(cumlog)[:, :, None] * jnp.einsum('tn,hpn->thp', c_c, carried, precision=highest)
        to_end = jnp.exp(cumlog[-1][None, :] - cumlog)
        weighted = to_end[:, :, None] * xdt_c
        fresh = jnp.einsum('shp,sn->hpn', weighted, b_c, precision=highest)
        updated = jnp.exp(cumlog[-1])[:, None, None] * carried + fresh
        return (updated, outputs)
    initial = jnp.zeros((HEADS, HEAD_DIM, STATE), jnp.float32)
    inputs = (log_decay.reshape(blocks, GROUP, HEADS), x_dt.reshape(blocks, GROUP, HEADS, HEAD_DIM), b_mat.reshape(blocks, GROUP, STATE), c_mat.reshape(blocks, GROUP, STATE))
    final_state, outputs = lax.scan(group_step, initial, inputs)
    y_heads = outputs.reshape(TOKENS, HEADS, HEAD_DIM) + skip_d[None, :, None] * x_heads
    gated = (y_heads * jax.nn.silu(gate_z.astype(jnp.float32))).astype(jnp.bfloat16).reshape(TOKENS, DINNER)
    gated_f = gated.astype(jnp.float32)
    mean_sq = lax.optimization_barrier(jnp.mean(gated_f * gated_f, axis=1, keepdims=True))
    normed = (gated_f * lax.rsqrt(mean_sq + epsilon) * norm_gain).astype(jnp.bfloat16)
    return jnp.dot(normed, w_out, preferred_element_type=jnp.float32).astype(jnp.bfloat16)
```

```python
import functools
import math

import jax
import jax.numpy as jnp
from jax import lax
from jax.experimental import pallas as pl
from jax.experimental.pallas import tpu as pltpu
from jax.sharding import PartitionSpec as P

HEADS = 32
HEAD_DIM = 64
STATE = 64
CONV = 4
QUADS = HEADS // 4
LANES = 4 * HEAD_DIM
HALF = 128
CHUNK = 128
HALO = 16
MSG = STATE + 16
EPSILON = 1e-05
LOG2E = math.log2(math.e)

f32, bf16 = jnp.float32, jnp.bfloat16
MESH = pl.DeviceIdType.MESH


def silu(x):
    half = 0.5 * x
    return half * (1.0 + jnp.tanh(half))


def dot(a, b, **kw):
    return jnp.dot(a, b, preferred_element_type=f32, **kw)


def iota(shape, dim):
    return lax.broadcasted_iota(jnp.int32, shape, dim)


def put(ref, at, state, factor):
    hi = factor.astype(bf16).astype(f32)
    first = iota((16, LANES), 0) < 8
    ref[(*at, pl.ds(0, STATE), slice(None))] = state.astype(bf16)
    ref[(*at, pl.ds(STATE, 16), slice(None))] = jnp.where(first, hi, factor - hi).astype(bf16)


def get(block):
    block = block.astype(f32)
    return block[:STATE], block[STATE : STATE + 1] + block[STATE + 8 : STATE + 9]


def group_of(n_seq):
    return 2 if n_seq % 2 == 0 else 1


def kernel(
    n_seq, n_head,
    tok_hbm, wg_hbm, wo_hbm, wbc_ref, cw_ref, cb_ref, cbcw_ref, cbcb_ref, dtb_ref, alog_ref, skip_ref, gain_ref,
    out_ref,
    tok, wbuf, wout, prm, bc_pad, bcv, cmat, bmat_t, six, cum_t, scores,
    xs, xbuf, xdt, cume, starts, msg, ybuf, gbuf,
    from_group, to_next, from_prev, to_group, sin,
    w_sem, l_sem, halo_sem, prm_sem, a_sem, b_sem, c_sem,
):
    T = tok_hbm.shape[0]
    n_chunk = T // CHUNK
    g_seq = group_of(n_seq)
    size, n_group = g_seq * n_head, n_seq // g_seq
    per = QUADS // size
    quads_in = QUADS // n_head
    here = HEADS // n_head
    seq, head = lax.axis_index("seq"), lax.axis_index("head")
    place, group = lax.rem(seq, g_seq) * n_head + head, seq // g_seq
    hops = [1 << k for k in range(n_group.bit_length()) if (1 << k) < n_group]

    def member(i):
        return (group * g_seq + i // n_head, lax.rem(i, n_head))

    wrap = head == n_head - 1
    next_device = (jnp.where(wrap, seq + 1, seq), jnp.where(wrap, 0, head + 1))
    has_next = jnp.logical_or(seq < n_seq - 1, head < n_head - 1)
    has_prev = jnp.logical_or(seq > 0, head > 0)

    tok_copy = pltpu.make_async_copy(tok_hbm, tok.at[pl.ds(HALO, T)], l_sem.at[0])
    tok_copy.start()

    def w_copy(q):
        cols = pl.ds(pl.multiple_of(q * 2 * LANES, 2 * LANES), 2 * LANES)
        return pltpu.make_async_copy(wg_hbm.at[:, cols], wbuf.at[q], w_sem.at[q])

    @pl.loop(0, QUADS)
    def _(q):
        w_copy(q).start()

    wo_copy = pltpu.make_async_copy(wo_hbm, wout, l_sem.at[1])
    wo_copy.start()

    barrier = pltpu.get_barrier_semaphore()

    def greet(cond, target):
        @pl.when(cond)
        def _():
            pl.semaphore_signal(barrier, inc=1, device_id=target, device_id_type=MESH)

    for o in range(1, size):
        pl.semaphore_signal(
            barrier, inc=1, device_id=member(lax.rem(place + o, size)), device_id_type=MESH
        )
    total = jnp.int32(size - 1)
    for d in hops:
        ahead, behind = group + d < n_group, group >= d
        greet(ahead, (seq + d * g_seq, head))
        greet(behind, (seq - d * g_seq, head))
        total = total + ahead.astype(jnp.int32) + behind.astype(jnp.int32)
    over = jnp.logical_and(place == size - 1, group < n_group - 1)
    under = jnp.logical_and(place == 0, group > 0)
    greet(over, (seq + 1, 0))
    greet(under, (seq - 1, n_head - 1))
    total = total + over.astype(jnp.int32) + under.astype(jnp.int32)

    wide = iota((1, LANES), 1)
    for k in range(quads_in):
        cols = slice(k * LANES, (k + 1) * LANES)
        at = head * quads_in + k
        prm[at, 0:CONV, :] = cw_ref[:, cols]
        prm[at, CONV : CONV + 1, :] = cb_ref[...].reshape(1, here * HEAD_DIM)[:, cols]
        skip = jnp.zeros((1, LANES), f32)
        vec_b, vec_a = skip, skip
        for i in range(4):
            skip = jnp.where(wide // HEAD_DIM == i, skip_ref[4 * k + i], skip)
        if k == 0:
            for i in range(here):
                mine = lax.rem(wide, HEADS) == head * here + i
                vec_b = jnp.where(mine, dtb_ref[i], vec_b)
                vec_a = jnp.where(mine, alog_ref[i], vec_a)
        prm[at, CONV + 1 : CONV + 2, :] = skip
        prm[at, CONV + 2 : CONV + 3, :] = vec_b
        prm[at, CONV + 3 : CONV + 4, :] = vec_a

    pl.semaphore_wait(barrier, total)

    def halo_copy():
        return pltpu.make_async_remote_copy(
            src_ref=tok_hbm.at[pl.ds(T - HALO, HALO)], dst_ref=tok.at[pl.ds(0, HALO)],
            send_sem=halo_sem.at[0], recv_sem=halo_sem.at[1],
            device_id=next_device, device_id_type=MESH,
        )

    @pl.when(has_next)
    def _():
        halo_copy().start()

    def prm_copy(o):
        block = prm.at[pl.ds(head * quads_in, quads_in)]
        return pltpu.make_async_remote_copy(
            src_ref=block, dst_ref=block,
            send_sem=prm_sem.at[0, o], recv_sem=prm_sem.at[1, o],
            device_id=(seq, lax.rem(head + o, n_head)), device_id_type=MESH,
        )

    for o in range(1, n_head):
        prm_copy(o).start()

    @pl.when(jnp.logical_not(has_prev))
    def _():
        tok[pl.ds(0, HALO), :] = jnp.zeros((HALO, tok.shape[1]), bf16)

    tok_copy.wait()

    @pl.when(has_prev)
    def _():
        halo_copy().wait_recv()

    @pl.when(has_next)
    def _():
        halo_copy().wait_send()

    for o in range(1, n_head):
        prm_copy(o).wait()

    w_dt = wbc_ref[2 * STATE :, :]
    w_bc = jnp.concatenate([wbc_ref[...], w_dt, w_dt, w_dt], axis=0)
    bc_dt = lax.dot_general(
        tok[...], w_bc, (((1,), (1,)), ((), ())), preferred_element_type=f32
    ).astype(bf16).astype(f32)
    bc_pad[...] = bc_dt[:, :HALF]
    acc = cbcb_ref[...].reshape(1, HALF)
    for k in range(CONV):
        acc = acc + cbcw_ref[pl.ds(k, 1), :] * bc_pad[pl.ds(HALO - CONV + 1 + k, T), :]
    bcv[...] = silu(acc).astype(bf16).astype(f32)
    head_prm = prm[0]
    for j in range(1, n_head):
        head_prm = head_prm + prm[j * quads_in]
    raw = bc_dt[HALO:, HALF:] + head_prm[CONV + 2 : CONV + 3, :HALF]
    dt = jnp.maximum(raw, 0.0) + jnp.log1p(jnp.exp(-jnp.abs(raw)))
    decay = dt * (-LOG2E * jnp.exp(head_prm[CONV + 3 : CONV + 4, :HALF]))

    def three(v):
        hi = v.astype(bf16).astype(f32)
        mid = (v - hi).astype(bf16).astype(f32)
        rest = v - hi - mid
        ln = iota(v.shape, 1)
        part = jnp.where(ln < 32, hi, jnp.where(ln < 64, mid, jnp.where(ln < 96, rest, 0.0)))
        return part.astype(bf16)

    six[:, 0:HALF] = three(dt)
    row, col = iota((CHUNK, CHUNK), 0), iota((CHUNK, CHUNK), 1)
    lower = row >= col
    tril = jnp.where(lower, 1.0, 0.0)
    for c in range(n_chunk):
        rows = slice(c * CHUNK, (c + 1) * CHUNK)
        cum = dot(tril, decay[rows], precision=lax.Precision.HIGHEST)
        six[rows, HALF:] = three(cum)
        cum_t[c] = cum.T
        both = bcv[rows, :]
        flipped = both.T
        bmat_t[:, rows] = flipped[:STATE].astype(bf16)
        c_c = both[:, STATE:].astype(bf16)
        cmat[rows, :] = c_c
        scores[c] = jnp.where(lower, dot(c_c, flipped[:STATE].astype(bf16)), 0.0)

    def half_of(q, first):
        cuts = [slice(2 * HEAD_DIM * i + first, 2 * HEAD_DIM * i + first + HEAD_DIM) for i in range(4)]
        return jnp.concatenate([wbuf[q, :, cut] for cut in cuts], axis=1)

    def a_copy(owner, slot):
        return pltpu.make_async_remote_copy(
            src_ref=msg.at[pl.ds(owner * per, per)], dst_ref=from_group.at[slot],
            send_sem=a_sem.at[0, owner], recv_sem=a_sem.at[1, slot],
            device_id=member(owner), device_id_type=MESH,
        )

    @pl.loop(0, QUADS)
    def _(q):
        w_copy(q).wait()
        pq = prm[q]
        xs[...] = dot(tok[...], half_of(q, HEAD_DIM)).astype(bf16).astype(f32)
        r6, l6 = iota((HALF, LANES), 0), iota((HALF, LANES), 1)
        spread = jnp.where((r6 & 31) == 4 * q + (l6 >> 6), 1.0, 0.0).astype(bf16)
        state = jnp.zeros((STATE, LANES), f32)
        whole = jnp.zeros((1, LANES), f32)
        for c in range(n_chunk):
            rows = slice(c * CHUNK, (c + 1) * CHUNK)
            acc = pq[CONV : CONV + 1]
            for k in range(CONV):
                acc = acc + pq[k : k + 1] * xs[pl.ds(HALO - CONV + 1 + k + c * CHUNK, CHUNK), :]
            xc = silu(acc).astype(bf16)
            xbuf[q, rows, :] = xc
            xd = xc.astype(f32) * dot(six[rows, :HALF], spread)
            ce = dot(six[rows, HALF:], spread)
            xdt[q, rows, :] = xd.astype(bf16)
            cume[q, rows, :] = ce
            end = ce[CHUNK - 1 : CHUNK]
            starts[q, c] = state.astype(bf16)
            weighted = (jnp.exp2(end - ce) * xd).astype(bf16)
            state = jnp.exp2(end) * state + dot(bmat_t[:, rows], weighted)
            whole = whole + end
        put(msg, (q,), state, jnp.exp2(whole))
        owner = q // per

        @pl.when(jnp.logical_and(lax.rem(q, per) == per - 1, owner != place))
        def _():
            a_copy(owner, place).start()

    from_group[place] = msg[pl.ds(place * per, per)]

    def intra(first, last):
        @pl.loop(first, last)
        def _(q):
            skip = prm[q, CONV + 1 : CONV + 2]
            w_z = half_of(q, 0)
            off = jnp.zeros((1, LANES), f32)
            for c in range(n_chunk):
                rows = pl.ds(c * CHUNK, CHUNK)
                z = dot(tok[pl.ds(HALO + c * CHUNK, CHUNK), :], w_z).astype(bf16).astype(f32)
                gate = silu(z)
                ce = cume[q, rows, :]
                s_c = scores[c]
                x_c = xdt[q, rows, :]
                y_parts = []
                for pair in range(2):
                    parts = []
                    for odd in range(2):
                        i = 2 * pair + odd
                        gap = ce[:, i * HEAD_DIM : i * HEAD_DIM + 1] - cum_t[c, pl.ds(4 * q + i, 1), :]
                        parts.append((s_c * jnp.exp2(jnp.minimum(gap, 0.0))).astype(bf16))
                    x_p = x_c[:, pair * HALF : (pair + 1) * HALF].astype(f32)
                    lo_c = iota(x_p.shape, 1) < HEAD_DIM
                    right = jnp.concatenate(
                        [jnp.where(lo_c, x_p, 0.0).astype(bf16), jnp.where(lo_c, 0.0, x_p).astype(bf16)], axis=0
                    )
                    y_parts.append(dot(jnp.concatenate(parts, axis=1), right))
                y = jnp.concatenate(y_parts, axis=1)
                y = y + jnp.exp2(ce) * dot(cmat[rows, :], starts[q, c])
                ybuf[q, rows, :] = (y + skip * xbuf[q, rows, :].astype(f32)) * gate
                cume[q, rows, :] = jnp.exp2(ce + off) * gate
                off = off + ce[CHUNK - 1 : CHUNK]

    slots = len(hops) + 2
    cuts = [QUADS * k // slots for k in range(slots + 1)]
    intra(cuts[0], cuts[1])

    for o in range(size):
        @pl.when(place != o)
        def _():
            a_copy(jnp.int32(o), o).wait()

    none = (jnp.zeros((STATE, LANES), f32), jnp.ones((1, LANES), f32))
    inc, before = [], []
    for p in range(per):
        state, factor = none
        mine = []
        for j in range(size):
            mine.append((state, factor))
            s_j, f_j = get(from_group[j, p])
            state, factor = f_j * state + s_j, factor * f_j
        before.append(mine)
        inc.append((state, factor))
    exc = [none for _ in range(per)]

    def b_copy(k):
        return pltpu.make_async_remote_copy(
            src_ref=to_next.at[k], dst_ref=from_prev.at[k],
            send_sem=b_sem.at[0, k], recv_sem=b_sem.at[1, k],
            device_id=(seq + hops[k] * g_seq, head), device_id_type=MESH,
        )

    for k, d in enumerate(hops):
        for p in range(per):
            put(to_next, (k, p), *inc[p])

        @pl.when(group + d < n_group)
        def _():
            b_copy(k).start()

        @pl.when(group < d)
        def _():
            for p in range(per):
                put(from_prev, (k, p), *none)

        intra(cuts[k + 1], cuts[k + 2])

        @pl.when(group >= d)
        def _():
            b_copy(k).wait_recv()

        @pl.when(group + d < n_group)
        def _():
            b_copy(k).wait_send()

        for p in range(per):
            s_r, f_r = get(from_prev[k, p])
            (s_i, f_i), (s_e, f_e) = inc[p], exc[p]
            inc[p] = (s_i + f_i * s_r, f_i * f_r)
            exc[p] = (s_e + f_e * s_r, f_e * f_r)

    for j in range(size):
        for p in range(per):
            s_b, f_b = before[p][j]
            to_group[j, p] = (s_b + f_b * exc[p][0]).astype(bf16)

    def c_copy(o, slot):
        return pltpu.make_async_remote_copy(
            src_ref=to_group.at[o], dst_ref=sin.at[slot],
            send_sem=c_sem.at[0, o], recv_sem=c_sem.at[1, slot],
            device_id=member(o), device_id_type=MESH,
        )

    for o in range(size):
        @pl.when(place != o)
        def _():
            c_copy(jnp.int32(o), place).start()

    sin[place] = to_group[place]
    intra(cuts[-2], cuts[-1])
    for o in range(size):
        @pl.when(place != o)
        def _():
            c_copy(jnp.int32(o), o).wait()

    def finish(q, squares):
        gated = ybuf[q] + cume[q] * dot(cmat[...], sin[q // per, lax.rem(q, per)])
        gated = gated.astype(bf16).astype(f32)
        cols = pl.ds(pl.multiple_of(q * LANES, LANES), LANES)
        gbuf[:, cols] = (gated * gain_ref[cols].reshape(1, LANES)).astype(bf16)
        squared = gated * gated
        return squares + squared[:, :HALF] + squared[:, HALF:]

    squares = lax.fori_loop(0, QUADS, finish, jnp.zeros((T, HALF), f32))
    mean_sq = jnp.sum(squares, axis=1, keepdims=True) * (1.0 / (HEADS * HEAD_DIM))
    scale = lax.rsqrt(mean_sq + EPSILON)
    wo_copy.wait()
    width = out_ref.shape[1]
    for n in range(width // 256):
        cols = slice(n * 256, (n + 1) * 256)
        out_ref[:, cols] = (dot(gbuf[...], wout[:, cols]) * scale).astype(bf16)


def on_device(
    n_seq, n_head,
    tokens, w_gate_x, w_bc_dt, conv_x_weight, conv_x_bias, conv_bc_weight, conv_bc_bias,
    dt_bias, a_log, skip_d, norm_gain, w_out,
):
    T, width = tokens.shape
    g_seq = group_of(n_seq)
    size = g_seq * n_head
    per = QUADS // size
    n_hops = max(1, (n_seq // g_seq - 1).bit_length())
    n_chunk = T // CHUNK
    vmem, any_ = pl.BlockSpec(memory_space=pltpu.VMEM), pl.BlockSpec(memory_space=pl.ANY)
    smem = pl.BlockSpec(memory_space=pltpu.SMEM)
    dma = pltpu.SemaphoreType.DMA
    return pl.pallas_call(
        functools.partial(kernel, n_seq, n_head),
        out_shape=jax.ShapeDtypeStruct((T, width), bf16),
        in_specs=[any_, any_, any_, vmem, vmem, vmem, vmem, vmem, smem, smem, smem, vmem],
        out_specs=vmem,
        scratch_shapes=[
            pltpu.VMEM((HALO + T, width), bf16),
            pltpu.VMEM((QUADS, width, 2 * LANES), bf16),
            pltpu.VMEM(w_out.shape, bf16),
            pltpu.VMEM((QUADS, 8, LANES), f32),
            pltpu.VMEM((HALO + T, HALF), f32),
            pltpu.VMEM((T, HALF), f32),
            pltpu.VMEM((T, STATE), bf16),
            pltpu.VMEM((STATE, T), bf16),
            pltpu.VMEM((T, 2 * HALF), bf16),
            pltpu.VMEM((n_chunk, HALF, CHUNK), f32),
            pltpu.VMEM((n_chunk, CHUNK, CHUNK), f32),
            pltpu.VMEM((HALO + T, LANES), f32),
            pltpu.VMEM((QUADS, T, LANES), bf16),
            pltpu.VMEM((QUADS, T, LANES), bf16),
            pltpu.VMEM((QUADS, T, LANES), f32),
            pltpu.VMEM((QUADS, n_chunk, STATE, LANES), bf16),
            pltpu.VMEM((QUADS, MSG, LANES), bf16),
            pltpu.VMEM((QUADS, T, LANES), f32),
            pltpu.VMEM((T, HEADS * HEAD_DIM), bf16),
            pltpu.VMEM((size, per, MSG, LANES), bf16),
            pltpu.VMEM((n_hops, per, MSG, LANES), bf16),
            pltpu.VMEM((n_hops, per, MSG, LANES), bf16),
            pltpu.VMEM((size, per, STATE, LANES), bf16),
            pltpu.VMEM((size, per, STATE, LANES), bf16),
            dma((QUADS,)),
            dma((2,)),
            dma((2,)),
            dma((2, n_head)),
            dma((2, size)),
            dma((2, n_hops)),
            dma((2, size)),
        ],
        compiler_params=pltpu.CompilerParams(
            collective_id=0, has_side_effects=True, vmem_limit_bytes=56 * 1024 * 1024
        ),
        cost_estimate=pl.CostEstimate(
            flops=2 * T * width * 6500, bytes_accessed=14 * 1024 * 1024, transcendentals=0
        ),
    )(
        tokens, w_gate_x, w_out, w_bc_dt.T, conv_x_weight, conv_x_bias, conv_bc_weight, conv_bc_bias,
        dt_bias, a_log, skip_d, norm_gain,
    )


def solution(mesh):
    return jax.shard_map(
        functools.partial(on_device, mesh.shape["seq"], mesh.shape["head"]),
        mesh=mesh,
        in_specs=(
            P(("seq", "head"), None),
            P(),
            P(),
            P(None, "head"),
            P("head"),
            P(),
            P(),
            P("head"),
            P("head"),
            P("head"),
            P(),
            P(),
        ),
        out_specs=P(("seq", "head"), None),
        check_vma=False,
    )
```

```python
import functools
import math

import jax
import jax.numpy as jnp
from jax import lax
from jax.experimental import pallas as pl
from jax.experimental.pallas import tpu as pltpu
from jax.sharding import PartitionSpec as P

HEADS = 32
HEAD_DIM = 64
STATE = 64
CONV = 4
QUADS = HEADS // 4
LANES = 4 * HEAD_DIM
HALF = 128
CHUNK = 128
HALO = 16
MSG = STATE + 16
EPSILON = 1e-05
LOG2E = math.log2(math.e)

f32, bf16 = jnp.float32, jnp.bfloat16
MESH = pl.DeviceIdType.MESH


def silu(x):
    half = 0.5 * x
    return half * (1.0 + jnp.tanh(half))


def dot(a, b, **kw):
    return jnp.dot(a, b, preferred_element_type=f32, **kw)


def iota(shape, dim):
    return lax.broadcasted_iota(jnp.int32, shape, dim)


def put(ref, at, state, factor):
    hi = factor.astype(bf16).astype(f32)
    first = iota((16, LANES), 0) < 8
    ref[(*at, pl.ds(0, STATE), slice(None))] = state.astype(bf16)
    ref[(*at, pl.ds(STATE, 16), slice(None))] = jnp.where(first, hi, factor - hi).astype(bf16)


def get(block):
    block = block.astype(f32)
    return block[:STATE], block[STATE : STATE + 1] + block[STATE + 8 : STATE + 9]


def group_of(n_seq):
    return 2 if n_seq % 2 == 0 else 1


def kernel(
    n_seq, n_head,
    tok_hbm, wg_hbm, wo_hbm, wbc_ref, cw_ref, cb_ref, cbcw_ref, cbcb_ref, dtb_ref, alog_ref, skip_ref, gain_ref,
    out_ref,
    tok, wbuf, wout, prm, bc_pad, bcv, cmat, bmat_t, six, cum_t, scores,
    buf_a, buf_b, zs_a, zs_b, xbuf, xdt, cume, starts, msg, ybuf, gbuf,
    from_group, to_next, from_prev, to_group, sin, before, run,
    w_sem, l_sem, halo_sem, prm_sem, a_sem, b_sem, c_sem,
):
    T = tok_hbm.shape[0]
    n_chunk = T // CHUNK
    g_seq = group_of(n_seq)
    size, n_group = g_seq * n_head, n_seq // g_seq
    per = QUADS // size
    quads_in = QUADS // n_head
    here = HEADS // n_head
    seq, head = lax.axis_index("seq"), lax.axis_index("head")
    place, group = lax.rem(seq, g_seq) * n_head + head, seq // g_seq
    hops = [1 << k for k in range(n_group.bit_length()) if (1 << k) < n_group]

    def member(i):
        return (group * g_seq + i // n_head, lax.rem(i, n_head))

    wrap = head == n_head - 1
    next_device = (jnp.where(wrap, seq + 1, seq), jnp.where(wrap, 0, head + 1))
    has_next = jnp.logical_or(seq < n_seq - 1, head < n_head - 1)
    has_prev = jnp.logical_or(seq > 0, head > 0)

    tok_copy = pltpu.make_async_copy(tok_hbm, tok.at[pl.ds(HALO, T)], l_sem.at[0])
    tok_copy.start()

    def w_copy(q):
        cols = pl.ds(pl.multiple_of(q * 2 * LANES, 2 * LANES), 2 * LANES)
        return pltpu.make_async_copy(wg_hbm.at[:, cols], wbuf.at[q], w_sem.at[q])

    @pl.loop(0, QUADS)
    def _(q):
        w_copy(q).start()

    wo_copy = pltpu.make_async_copy(wo_hbm, wout, l_sem.at[1])
    wo_copy.start()

    barrier = pltpu.get_barrier_semaphore()

    def greet(cond, target):
        @pl.when(cond)
        def _():
            pl.semaphore_signal(barrier, inc=1, device_id=target, device_id_type=MESH)

    for o in range(1, size):
        pl.semaphore_signal(
            barrier, inc=1, device_id=member(lax.rem(place + o, size)), device_id_type=MESH
        )
    total = jnp.int32(size - 1)
    for d in hops:
        ahead, behind = group + d < n_group, group >= d
        greet(ahead, (seq + d * g_seq, head))
        greet(behind, (seq - d * g_seq, head))
        total = total + ahead.astype(jnp.int32) + behind.astype(jnp.int32)
    over = jnp.logical_and(place == size - 1, group < n_group - 1)
    under = jnp.logical_and(place == 0, group > 0)
    greet(over, (seq + 1, 0))
    greet(under, (seq - 1, n_head - 1))
    total = total + over.astype(jnp.int32) + under.astype(jnp.int32)

    wide = iota((1, LANES), 1)
    for k in range(quads_in):
        cols = slice(k * LANES, (k + 1) * LANES)
        at = head * quads_in + k
        prm[at, 0:CONV, :] = cw_ref[:, cols]
        prm[at, CONV : CONV + 1, :] = cb_ref[...].reshape(1, here * HEAD_DIM)[:, cols]
        skip = jnp.zeros((1, LANES), f32)
        vec_b, vec_a = skip, skip
        for i in range(4):
            skip = jnp.where(wide // HEAD_DIM == i, skip_ref[4 * k + i], skip)
        if k == 0:
            for i in range(here):
                mine = lax.rem(wide, HEADS) == head * here + i
                vec_b = jnp.where(mine, dtb_ref[i], vec_b)
                vec_a = jnp.where(mine, alog_ref[i], vec_a)
        prm[at, CONV + 1 : CONV + 2, :] = skip
        prm[at, CONV + 2 : CONV + 3, :] = vec_b
        prm[at, CONV + 3 : CONV + 4, :] = vec_a

    pl.semaphore_wait(barrier, total)

    def halo_copy():
        return pltpu.make_async_remote_copy(
            src_ref=tok_hbm.at[pl.ds(T - HALO, HALO)], dst_ref=tok.at[pl.ds(0, HALO)],
            send_sem=halo_sem.at[0], recv_sem=halo_sem.at[1],
            device_id=next_device, device_id_type=MESH,
        )

    @pl.when(has_next)
    def _():
        halo_copy().start()

    def prm_copy(o):
        block = prm.at[pl.ds(head * quads_in, quads_in)]
        return pltpu.make_async_remote_copy(
            src_ref=block, dst_ref=block,
            send_sem=prm_sem.at[0, o], recv_sem=prm_sem.at[1, o],
            device_id=(seq, lax.rem(head + o, n_head)), device_id_type=MESH,
        )

    for o in range(1, n_head):
        prm_copy(o).start()

    @pl.when(jnp.logical_not(has_prev))
    def _():
        tok[pl.ds(0, HALO), :] = jnp.zeros((HALO, tok.shape[1]), bf16)

    tok_copy.wait()

    @pl.when(has_prev)
    def _():
        halo_copy().wait_recv()

    @pl.when(has_next)
    def _():
        halo_copy().wait_send()

    for o in range(1, n_head):
        prm_copy(o).wait()

    w_dt = wbc_ref[2 * STATE :, :]
    w_bc = jnp.concatenate([wbc_ref[...], w_dt, w_dt, w_dt], axis=0)
    bc_dt = lax.dot_general(
        tok[...], w_bc, (((1,), (1,)), ((), ())), preferred_element_type=f32
    ).astype(bf16).astype(f32)
    bc_pad[...] = bc_dt[:, :HALF]
    acc = cbcb_ref[...].reshape(1, HALF)
    for k in range(CONV):
        acc = acc + cbcw_ref[pl.ds(k, 1), :] * bc_pad[pl.ds(HALO - CONV + 1 + k, T), :]
    bcv[...] = silu(acc).astype(bf16).astype(f32)
    head_prm = prm[0]
    for j in range(1, n_head):
        head_prm = head_prm + prm[j * quads_in]
    raw = bc_dt[HALO:, HALF:] + head_prm[CONV + 2 : CONV + 3, :HALF]
    dt = jnp.maximum(raw, 0.0) + jnp.log1p(jnp.exp(-jnp.abs(raw)))
    decay = dt * (-LOG2E * jnp.exp(head_prm[CONV + 3 : CONV + 4, :HALF]))

    def three(v):
        hi = v.astype(bf16).astype(f32)
        mid = (v - hi).astype(bf16).astype(f32)
        rest = v - hi - mid
        ln = iota(v.shape, 1)
        part = jnp.where(ln < 32, hi, jnp.where(ln < 64, mid, jnp.where(ln < 96, rest, 0.0)))
        return part.astype(bf16)

    six[:, 0:HALF] = three(dt)
    row, col = iota((CHUNK, CHUNK), 0), iota((CHUNK, CHUNK), 1)
    lower = row >= col
    tril = jnp.where(lower, 1.0, 0.0)
    for c in range(n_chunk):
        rows = slice(c * CHUNK, (c + 1) * CHUNK)
        cum = dot(tril, decay[rows], precision=lax.Precision.HIGHEST)
        six[rows, HALF:] = three(cum)
        cum_t[c] = cum.T
        both = bcv[rows, :]
        flipped = both.T
        bmat_t[:, rows] = flipped[:STATE].astype(bf16)
        c_c = both[:, STATE:].astype(bf16)
        cmat[rows, :] = c_c
        scores[c] = jnp.where(lower, dot(c_c, flipped[:STATE].astype(bf16)), 0.0)

    def half_of(q, first):
        cuts = [slice(2 * HEAD_DIM * i + first, 2 * HEAD_DIM * i + first + HEAD_DIM) for i in range(4)]
        return jnp.concatenate([wbuf[q, :, cut] for cut in cuts], axis=1)

    def a_copy(owner, slot):
        return pltpu.make_async_remote_copy(
            src_ref=msg.at[pl.ds(owner * per, per)], dst_ref=from_group.at[slot],
            send_sem=a_sem.at[0, owner], recv_sem=a_sem.at[1, slot],
            device_id=member(owner), device_id_type=MESH,
        )

    def project_x(q, xs):
        w_copy(q).wait()
        xs[...] = dot(tok[...], half_of(q, HEAD_DIM)).astype(bf16).astype(f32)

    def project_z(q, zs):
        zs[...] = dot(tok[pl.ds(HALO, T), :], half_of(q, 0)).astype(bf16).astype(f32)

    def states(q, xs):
        pq = prm[q]
        r6, l6 = iota((HALF, LANES), 0), iota((HALF, LANES), 1)
        spread = jnp.where((r6 & 31) == 4 * q + (l6 >> 6), 1.0, 0.0).astype(bf16)
        steps = dot(six[:, :HALF], spread)
        cums = dot(six[:, HALF:], spread)
        cume[q] = cums
        state = jnp.zeros((STATE, LANES), f32)
        whole = jnp.zeros((1, LANES), f32)
        for c in range(n_chunk):
            rows = slice(c * CHUNK, (c + 1) * CHUNK)
            acc = pq[CONV : CONV + 1]
            for k in range(CONV):
                acc = acc + pq[k : k + 1] * xs[pl.ds(HALO - CONV + 1 + k + c * CHUNK, CHUNK), :]
            xc = silu(acc).astype(bf16)
            xbuf[q, rows, :] = xc
            xd = xc.astype(f32) * steps[rows]
            ce = cums[rows]
            xdt[q, rows, :] = xd.astype(bf16)
            end = ce[CHUNK - 1 : CHUNK]
            starts[q, c] = state.astype(bf16)
            weighted = (jnp.exp2(end - ce) * xd).astype(bf16)
            state = jnp.exp2(end) * state + dot(bmat_t[:, rows], weighted)
            whole = whole + end
        put(msg, (q,), state, jnp.exp2(whole))

    def intra(q, zs):
        skip = prm[q, CONV + 1 : CONV + 2]
        off = jnp.zeros((1, LANES), f32)
        for c in range(n_chunk):
            rows = pl.ds(c * CHUNK, CHUNK)
            gate = silu(zs[rows, :])
            ce = cume[q, rows, :]
            s_c = scores[c]
            x_c = xdt[q, rows, :]
            y_parts = []
            for pair in range(2):
                parts = []
                for odd in range(2):
                    i = 2 * pair + odd
                    gap = ce[:, i * HEAD_DIM : i * HEAD_DIM + 1] - cum_t[c, pl.ds(4 * q + i, 1), :]
                    parts.append((s_c * jnp.exp2(jnp.minimum(gap, 0.0))).astype(bf16))
                x_p = x_c[:, pair * HALF : (pair + 1) * HALF].astype(f32)
                lo_c = iota(x_p.shape, 1) < HEAD_DIM
                right = jnp.concatenate(
                    [jnp.where(lo_c, x_p, 0.0).astype(bf16), jnp.where(lo_c, 0.0, x_p).astype(bf16)], axis=0
                )
                y_parts.append(dot(jnp.concatenate(parts, axis=1), right))
            y = jnp.concatenate(y_parts, axis=1)
            y = y + jnp.exp2(ce) * dot(cmat[rows, :], starts[q, c])
            ybuf[q, rows, :] = (y + skip * xbuf[q, rows, :].astype(f32)) * gate
            cume[q, rows, :] = jnp.exp2(ce + off) * gate
            off = off + ce[CHUNK - 1 : CHUNK]

    def b_copy(k):
        return pltpu.make_async_remote_copy(
            src_ref=to_next.at[k], dst_ref=from_prev.at[k],
            send_sem=b_sem.at[0, k], recv_sem=b_sem.at[1, k],
            device_id=(seq + hops[k] * g_seq, head), device_id_type=MESH,
        )

    def c_copy(o, slot):
        return pltpu.make_async_remote_copy(
            src_ref=to_group.at[o], dst_ref=sin.at[slot],
            send_sem=c_sem.at[0, o], recv_sem=c_sem.at[1, slot],
            device_id=member(o), device_id_type=MESH,
        )

    none = (jnp.zeros((STATE, LANES), f32), jnp.ones((1, LANES), f32))

    def scan_step(step):
        if step == 0:
            from_group[place] = msg[pl.ds(place * per, per)]
            for o in range(size):
                @pl.when(place != o)
                def _():
                    a_copy(jnp.int32(o), o).wait_recv()

            for p in range(per):
                state, factor = none
                for j in range(size):
                    before[j, p, 0:STATE, :] = state
                    before[j, p, pl.ds(STATE, 8), :] = jnp.broadcast_to(factor, (8, LANES))
                    s_j, f_j = get(from_group[j, p])
                    state, factor = f_j * state + s_j, factor * f_j
                total = (state, factor)
                for at, (s, f) in ((0, total), (1, none)):
                    run[at, p, 0:STATE, :] = s
                    run[at, p, pl.ds(STATE, 8), :] = jnp.broadcast_to(f, (8, LANES))
        else:
            k = step - 1

            @pl.when(group >= hops[k])
            def _():
                b_copy(k).wait_recv()

            @pl.when(group + hops[k] < n_group)
            def _():
                b_copy(k).wait_send()

            for p in range(per):
                s_r, f_r = get(from_prev[k, p])
                for at in range(2):
                    f = run[at, p, pl.ds(STATE, 1), :]
                    run[at, p, 0:STATE, :] = run[at, p, 0:STATE, :] + f * s_r
                    run[at, p, pl.ds(STATE, 8), :] = jnp.broadcast_to(f * f_r, (8, LANES))
        if step < len(hops):
            d = hops[step]
            for p in range(per):
                put(to_next, (step, p), run[0, p, 0:STATE, :], run[0, p, pl.ds(STATE, 1), :])

            @pl.when(group + d < n_group)
            def _():
                b_copy(step).start()

            @pl.when(group < d)
            def _():
                for p in range(per):
                    put(from_prev, (step, p), *none)
        else:
            for j in range(size):
                for p in range(per):
                    f_b = before[j, p, pl.ds(STATE, 1), :]
                    value = before[j, p, 0:STATE, :] + f_b * run[1, p, 0:STATE, :]
                    to_group[j, p] = value.astype(bf16)
            for o in range(size):
                @pl.when(place != o)
                def _():
                    c_copy(jnp.int32(o), place).start()

            sin[place] = to_group[place]

    ready = ((place + 1) * per - 1) // 2

    def scan_steps(slot):
        for step in range(len(hops) + 1):
            @pl.when(slot == ready + 1 + step)
            def _():
                scan_step(step)

    def send_states(i):
        for k in range(2):
            q = 2 * i + k
            owner = q // per

            @pl.when(jnp.logical_and(lax.rem(q, per) == per - 1, owner != place))
            def _():
                a_copy(owner, place).start()

    n_body = QUADS // 2
    project_x(0, buf_a)

    @pl.loop(0, n_body - 1)
    def _(i):
        project_x(2 * i + 1, buf_b)
        states(2 * i, buf_a)
        project_x(2 * i + 2, buf_a)
        states(2 * i + 1, buf_b)
        send_states(i)
        scan_steps(i)

    project_x(QUADS - 1, buf_b)
    states(QUADS - 2, buf_a)
    project_z(0, zs_a)
    states(QUADS - 1, buf_b)
    send_states(n_body - 1)
    scan_steps(n_body - 1)

    @pl.loop(0, n_body - 1)
    def _(i):
        project_z(2 * i + 1, zs_b)
        intra(2 * i, zs_a)
        project_z(2 * i + 2, zs_a)
        intra(2 * i + 1, zs_b)
        scan_steps(n_body + i)

    project_z(QUADS - 1, zs_b)
    intra(QUADS - 2, zs_a)
    intra(QUADS - 1, zs_b)
    for late in range(2 * n_body - 1, n_body + len(hops) + 1):
        scan_steps(late)
    for o in range(size):
        @pl.when(place != o)
        def _():
            a_copy(jnp.int32(o), o).wait_send()
            c_copy(jnp.int32(o), o).wait()

    def finish(q, squares):
        gated = ybuf[q] + cume[q] * dot(cmat[...], sin[q // per, lax.rem(q, per)])
        gated = gated.astype(bf16).astype(f32)
        cols = pl.ds(pl.multiple_of(q * LANES, LANES), LANES)
        gbuf[:, cols] = (gated * gain_ref[cols].reshape(1, LANES)).astype(bf16)
        squared = gated * gated
        return squares + squared[:, :HALF] + squared[:, HALF:]

    squares = lax.fori_loop(0, QUADS, finish, jnp.zeros((T, HALF), f32))
    mean_sq = jnp.sum(squares, axis=1, keepdims=True) * (1.0 / (HEADS * HEAD_DIM))
    scale = lax.rsqrt(mean_sq + EPSILON)
    wo_copy.wait()
    width = out_ref.shape[1]
    for n in range(width // 256):
        cols = slice(n * 256, (n + 1) * 256)
        out_ref[:, cols] = (dot(gbuf[...], wout[:, cols]) * scale).astype(bf16)


def on_device(
    n_seq, n_head,
    tokens, w_gate_x, w_bc_dt, conv_x_weight, conv_x_bias, conv_bc_weight, conv_bc_bias,
    dt_bias, a_log, skip_d, norm_gain, w_out,
):
    T, width = tokens.shape
    g_seq = group_of(n_seq)
    size = g_seq * n_head
    per = QUADS // size
    n_hops = max(1, (n_seq // g_seq - 1).bit_length())
    n_chunk = T // CHUNK
    vmem, any_ = pl.BlockSpec(memory_space=pltpu.VMEM), pl.BlockSpec(memory_space=pl.ANY)
    smem = pl.BlockSpec(memory_space=pltpu.SMEM)
    dma = pltpu.SemaphoreType.DMA
    return pl.pallas_call(
        functools.partial(kernel, n_seq, n_head),
        out_shape=jax.ShapeDtypeStruct((T, width), bf16),
        in_specs=[any_, any_, any_, vmem, vmem, vmem, vmem, vmem, smem, smem, smem, vmem],
        out_specs=vmem,
        scratch_shapes=[
            pltpu.VMEM((HALO + T, width), bf16),
            pltpu.VMEM((QUADS, width, 2 * LANES), bf16),
            pltpu.VMEM(w_out.shape, bf16),
            pltpu.VMEM((QUADS, 8, LANES), f32),
            pltpu.VMEM((HALO + T, HALF), f32),
            pltpu.VMEM((T, HALF), f32),
            pltpu.VMEM((T, STATE), bf16),
            pltpu.VMEM((STATE, T), bf16),
            pltpu.VMEM((T, 2 * HALF), bf16),
            pltpu.VMEM((n_chunk, HALF, CHUNK), f32),
            pltpu.VMEM((n_chunk, CHUNK, CHUNK), f32),
            pltpu.VMEM((HALO + T, LANES), f32),
            pltpu.VMEM((HALO + T, LANES), f32),
            pltpu.VMEM((T, LANES), f32),
            pltpu.VMEM((T, LANES), f32),
            pltpu.VMEM((QUADS, T, LANES), bf16),
            pltpu.VMEM((QUADS, T, LANES), bf16),
            pltpu.VMEM((QUADS, T, LANES), f32),
            pltpu.VMEM((QUADS, n_chunk, STATE, LANES), bf16),
            pltpu.VMEM((QUADS, MSG, LANES), bf16),
            pltpu.VMEM((QUADS, T, LANES), f32),
            pltpu.VMEM((T, HEADS * HEAD_DIM), bf16),
            pltpu.VMEM((size, per, MSG, LANES), bf16),
            pltpu.VMEM((n_hops, per, MSG, LANES), bf16),
            pltpu.VMEM((n_hops, per, MSG, LANES), bf16),
            pltpu.VMEM((size, per, STATE, LANES), bf16),
            pltpu.VMEM((size, per, STATE, LANES), bf16),
            pltpu.VMEM((size, per, STATE + 8, LANES), f32),
            pltpu.VMEM((2, per, STATE + 8, LANES), f32),
            dma((QUADS,)),
            dma((2,)),
            dma((2,)),
            dma((2, n_head)),
            dma((2, size)),
            dma((2, n_hops)),
            dma((2, size)),
        ],
        compiler_params=pltpu.CompilerParams(
            collective_id=0, has_side_effects=True, vmem_limit_bytes=56 * 1024 * 1024
        ),
        cost_estimate=pl.CostEstimate(
            flops=2 * T * width * 6500, bytes_accessed=14 * 1024 * 1024, transcendentals=0
        ),
    )(
        tokens, w_gate_x, w_out, w_bc_dt.T, conv_x_weight, conv_x_bias, conv_bc_weight, conv_bc_bias,
        dt_bias, a_log, skip_d, norm_gain,
    )


def solution(mesh):
    return jax.shard_map(
        functools.partial(on_device, mesh.shape["seq"], mesh.shape["head"]),
        mesh=mesh,
        in_specs=(
            P(("seq", "head"), None),
            P(),
            P(),
            P(None, "head"),
            P("head"),
            P(),
            P(),
            P("head"),
            P("head"),
            P("head"),
            P(),
            P(),
        ),
        out_specs=P(("seq", "head"), None),
        check_vma=False,
    )
```
